512 devices in a mesh: dp: 4 (over x), row: 8 (over y, core), col: 16 (over z).
Axes of the slice: x: 4, y: 4, z: 16, core: 2. Of those that a mesh axis runs over, the one named last changes fastest.
Arguments:
- tokens: bfloat16 [2048, 6144], P(('dp', 'col'), 'row'), may hold values from -6 to 6
- weight_up: bfloat16 [6144, 24576], P('row', 'col'), may hold values from -0.078125 to 0.078125
- d_hidden: bfloat16 [2048, 24576], P(('dp', 'row'), 'col'), may hold values from -0.796875 to 0.796875
Outputs:
- d_tokens: bfloat16 [2048, 6144], P(('dp', 'col'), 'row')
- d_weight: bfloat16 [6144, 24576], P('row', 'col')
The draws below stay inside these ranges and needn't reach their ends.
All inputs are finite; a program needn't handle non-finite values.
Results may differ from the reference program's by a relative error of at most 0.027.
Values may be sent and summed in bfloat16 or wider, within the bound.
No kernel may reach another device: no remote copies, remote signals or barrier semaphores. Data moves between devices by JAX's collectives and lax.ppermute only.
A program may use at most 64 MiB of HBM per device.

```python
import jax
import jax.numpy as jnp

D = 6144
FF = 24576
TOK = 512
TOKENS = 2048
N_DP = 4
N_COL = 16


def steps_of(stream_key, extent, pieces, least, high):
    loudness, own = 1.0, jax.random.fold_in(stream_key, 6)
    for axis_at, blocks in pieces:
        heights = jnp.exp(jax.random.uniform(jax.random.fold_in(own, axis_at), (blocks,), jnp.float32, least / len(pieces), high / len(pieces)))
        loudness = loudness * jnp.repeat(heights, extent[axis_at] // blocks).reshape([-1 if axis == axis_at else 1 for axis in range(len(extent))])
    return loudness


def gaussian(stream_key, extent, spread, most, pieces=(), dtype=jnp.bfloat16):
    values = spread * jax.random.normal(stream_key, extent, jnp.float32)
    if pieces:
        values = values * steps_of(stream_key, extent, pieces, -0.22, 0.18)
    return jnp.clip(values, -most, most).astype(dtype)


def setup_inputs(seed: int = 0) -> dict:
    keys = jax.random.split(jax.random.key(seed), 4)
    tokens = gaussian(keys[0], (TOKENS, D), 1.0, 6.0, ((0, 64), (1, 8)))
    weight_up = gaussian(keys[1], (D, FF), D ** -0.5, 0.078125, ((0, 8), (1, 16)))
    d_hidden = gaussian(keys[2], (TOKENS, FF), 0.1, 0.796875, ((0, 32), (1, 16)))
    return {"tokens": tokens, "weight_up": weight_up, "d_hidden": d_hidden}


def gelu_back(pre, cot):
    value, pullback = jax.vjp(lambda v: jax.nn.gelu(v, approximate=True), pre)
    return pullback(cot.astype(jnp.float32))[0].astype(jnp.bfloat16)

def reference(tokens, weight_up, d_hidden):
    block = FF // N_COL
    grad_rows = []
    weight_total = jnp.zeros((D, FF), jnp.float32)
    for group in range(N_DP):
        inputs = tokens[group * TOK:(group + 1) * TOK]
        cotan = d_hidden[group * TOK:(group + 1) * TOK]
        pre = jnp.dot(inputs, weight_up, preferred_element_type=jnp.float32)
        d_pre = gelu_back(pre, cotan)
        total = jnp.zeros((TOK, D), jnp.float32)
        for piece in range(N_COL):
            part = jnp.dot(d_pre[:, piece * block:(piece + 1) * block], weight_up[:, piece * block:(piece + 1) * block].T, preferred_element_type=jnp.float32)
            total = total + part.astype(jnp.bfloat16).astype(jnp.float32)
        grad_rows.append(total.astype(jnp.bfloat16))
        local = jnp.dot(inputs.T, d_pre, preferred_element_type=jnp.float32)
        weight_total = weight_total + local.astype(jnp.bfloat16).astype(jnp.float32)
    return (jnp.concatenate(grad_rows, axis=0), weight_total.astype(jnp.bfloat16))
```

```python
import functools

import jax
import jax.numpy as jnp
from jax import lax
from jax.experimental import pallas as pl
from jax.experimental.pallas import tpu as pltpu
from jax.sharding import PartitionSpec as P

F32 = jnp.float32
BF16 = jnp.bfloat16
VMEM_LIMIT = 24 * 1024 * 1024


def gelu_back(pre, cot):
    value, pullback = jax.vjp(lambda v: jax.nn.gelu(v, approximate=True), pre)
    return pullback(cot.astype(F32))[0].astype(BF16)


def shift(n, step):
    return [(i, (i + step) % n) for i in range(n)]


def tokens_kernel(where, own, other, w, plus, minus, across, keep, rows):
    core, k = where[0], where[1]
    n_y, per_row, width = own.shape
    half = per_row // 2
    block = n_y * half
    for i, step in enumerate((1, 3, 2, 0)):
        cls = lax.rem(k + step, 4)
        at = pl.ds(pl.multiple_of(lax.rem(cls, 2) * half, half), half)

        @pl.when(cls // 2 == core)
        def _():
            rows[pl.ds(i * block, block), :] = own[:, at, :].reshape(block, width)

        @pl.when(cls // 2 != core)
        def _():
            rows[pl.ds(i * block, block), :] = other[:, at, :].reshape(block, width)

    step = 256
    for n in range(w.shape[0] // step):
        cols = pl.ds(n * step, step)
        out = lax.dot_general(
            rows[...], w[cols, :], (((1,), (1,)), ((), ())), preferred_element_type=F32
        )
        plus[:, cols] = out[:block].astype(BF16)
        minus[:, cols] = out[block : 2 * block].astype(BF16)
        across[:, cols] = out[2 * block : 3 * block].astype(BF16)
        keep[:, cols] = out[3 * block :]


def tokens_parts(where, own, other, w):
    n_y, per_row, width = own.shape
    block, depth = n_y * per_row // 2, w.shape[0]
    vmem = pl.BlockSpec(memory_space=pltpu.VMEM)
    return pl.pallas_call(
        tokens_kernel,
        out_shape=[jax.ShapeDtypeStruct((block, depth), t) for t in (BF16, BF16, BF16, F32)],
        in_specs=[pl.BlockSpec(memory_space=pltpu.SMEM), vmem, vmem, vmem],
        out_specs=[vmem] * 4,
        scratch_shapes=[pltpu.VMEM((4 * block, width), BF16)],
        compiler_params=pltpu.CompilerParams(vmem_limit_bytes=VMEM_LIMIT),
        cost_estimate=pl.CostEstimate(
            flops=8 * block * width * depth, bytes_accessed=6 * 1024 * 1024, transcendentals=0
        ),
        name="tokens_parts",
    )(where, own, other, w)


def weight_kernel(which, has_add, where, t_all, own, up, far_a, far_b, down, *rest):
    out = rest[-1]
    n_dp = t_all.shape[0]
    dp = where[2]
    far = jnp.concatenate([far_a[...], far_b[...]], axis=0)
    total = None
    for step, g in ((0, own[...]), (1, up[...]), (2, far), (3, down[...])):
        t = t_all[step, which]
        part = lax.dot_general(t, g, (((0,), (0,)), ((), ())), preferred_element_type=F32)
        total = part if total is None else total + part
    if has_add:
        total = total + rest[0][...].astype(F32)
    out[...] = total.astype(BF16)


def weight_part(where, t_all, own, up, far_a, far_b, down, which, add=None):
    n_dp, _, tok, depth = t_all.shape
    width = own.shape[1]
    step = 512
    cut = lambda a: pl.BlockSpec((a.shape[0], step), lambda n: (0, n))
    operands = [own, up, far_a, far_b, down] + ([] if add is None else [add])
    return pl.pallas_call(
        functools.partial(weight_kernel, which, add is not None),
        grid=(width // step,),
        out_shape=jax.ShapeDtypeStruct((depth, width), BF16),
        in_specs=[
            pl.BlockSpec(memory_space=pltpu.SMEM),
            pl.BlockSpec(t_all.shape, lambda n: (0, 0, 0, 0)),
            *[cut(a) for a in operands],
        ],
        out_specs=pl.BlockSpec((depth, step), lambda n: (0, n)),
        compiler_params=pltpu.CompilerParams(vmem_limit_bytes=VMEM_LIMIT),
        cost_estimate=pl.CostEstimate(
            flops=2 * n_dp * tok * width * depth, bytes_accessed=8 * 1024 * 1024, transcendentals=0
        ),
        name="weight_part",
    )(where, t_all, *operands)


def per_device(tokens, weight_up, d_hidden):
    n_dp, n_row, n_col = lax.axis_size("dp"), lax.axis_size("row"), lax.axis_size("col")
    n_y = n_row // 2
    depth, width = weight_up.shape
    core = lax.axis_index("row") % 2
    col = lax.axis_index("col")
    other_core = [(i, i ^ 1) for i in range(n_row)]
    y_groups = [[2 * y + c for y in range(n_y)] for c in range(2)]
    where = jnp.stack([core, col % 4, lax.axis_index("dp")]).astype(jnp.int32)

    w_other = lax.ppermute(weight_up, "row", other_core)
    panel = lax.all_gather(tokens, "col", axis=0, tiled=True)
    per_row = panel.shape[0] // n_row
    split = panel.reshape(n_y, 2, per_row, depth)
    mine = lax.dynamic_index_in_dim(split, core, 1, keepdims=False).reshape(-1, depth)
    theirs = lax.dynamic_index_in_dim(split, 1 - core, 1, keepdims=False).reshape(-1, depth)
    swapped = lax.ppermute(theirs, "row", other_core)
    pair = jnp.stack([mine, swapped])
    t_up = lax.ppermute(pair, "dp", shift(n_dp, 1))
    t_down = lax.ppermute(pair, "dp", shift(n_dp, -1))

    chip = jnp.dot(mine, weight_up, preferred_element_type=F32)
    chip = chip + jnp.dot(swapped, w_other, preferred_element_type=F32)
    parts = lax.all_to_all(
        chip.astype(BF16), "row", 0, 0, tiled=True, axis_index_groups=y_groups
    )
    pre = parts.reshape(n_y, per_row, width).astype(F32).sum(0)
    grad = gelu_back(pre, d_hidden)

    own = lax.all_gather(grad, "row", axis=0, tiled=True, axis_index_groups=y_groups)
    other = lax.ppermute(own, "row", other_core)
    up = lax.ppermute(own, "dp", shift(n_dp, 1))
    down = lax.ppermute(own, "dp", shift(n_dp, -1))

    plus, minus, across, keep = tokens_parts(
        where, own.reshape(n_y, per_row, width), other.reshape(n_y, per_row, width), weight_up
    )
    plus = lax.ppermute(plus, "col", shift(n_col, 1))
    minus = lax.ppermute(minus, "col", shift(n_col, -1))
    across = lax.ppermute(across, "col", [(i, i ^ 2) for i in range(n_col)])
    quad = (keep + plus.astype(F32) + minus.astype(F32) + across.astype(F32)).astype(BF16)

    up, down, quad = lax.optimization_barrier((up, down, quad))
    t_up, t_down = lax.optimization_barrier((t_up, t_down))
    t_far = jnp.stack([
        lax.ppermute(t_up[0], "dp", shift(n_dp, 1)),
        lax.ppermute(t_down[1], "dp", shift(n_dp, -1)),
    ])
    t_all = jnp.stack([pair, t_up, t_far, t_down])
    halves = own.shape[0] // 2
    far_a = lax.ppermute(up[:halves], "dp", shift(n_dp, 1))
    far_b = lax.ppermute(down[halves:], "dp", shift(n_dp, -1))

    col_groups = [[c + 4 * q for q in range(n_col // 4)] for c in range(4)]
    parts = lax.all_to_all(quad, "col", 0, 0, tiled=True, axis_index_groups=col_groups)

    g = (own, up, far_a, far_b, down)
    away = lax.ppermute(weight_part(where, t_all, *g, 1), "row", other_core)
    here = weight_part(where, t_all, *g, 0)
    parts, here = lax.optimization_barrier((parts, here))
    d_tokens = parts.reshape(n_col // 4, -1, depth).astype(F32).sum(0).astype(BF16)
    d_weight = (here.astype(F32) + away.astype(F32)).astype(BF16)
    return d_tokens, d_weight


def solution(mesh):
    placed = (P(("dp", "col"), "row"), P("row", "col"), P(("dp", "row"), "col"))
    return jax.shard_map(
        per_device,
        mesh=mesh,
        in_specs=placed,
        out_specs=(P(("dp", "col"), "row"), P("row", "col")),
        check_vma=False,
    )
```

```python
import functools

import jax
import jax.numpy as jnp
from jax import lax
from jax.experimental import pallas as pl
from jax.experimental.pallas import tpu as pltpu
from jax.sharding import PartitionSpec as P

F32 = jnp.float32
BF16 = jnp.bfloat16
VMEM_LIMIT = 56 * 1024 * 1024
TOKENS_VMEM = 24 * 1024 * 1024


def gelu_back(pre, cot):
    value, pullback = jax.vjp(lambda v: jax.nn.gelu(v, approximate=True), pre)
    return pullback(cot.astype(F32))[0].astype(BF16)


def shift(n, step):
    return [(i, (i + step) % n) for i in range(n)]


together = lax.optimization_barrier


def tokens_kernel(where, own, other, w, plus, minus, across, keep, rows):
    core, k = where[0], where[1]
    n_y, per_row, width = own.shape
    half = per_row // 2
    block = n_y * half

    @pl.when(pl.program_id(0) == 0)
    def _():
        for i, step in enumerate((1, 3, 2, 0)):
            cls = lax.rem(k + step, 4)
            at = pl.ds(pl.multiple_of(lax.rem(cls, 2) * half, half), half)

            @pl.when(cls // 2 == core)
            def _():
                rows[pl.ds(i * block, block), :] = own[:, at, :].reshape(block, width)

            @pl.when(cls // 2 != core)
            def _():
                rows[pl.ds(i * block, block), :] = other[:, at, :].reshape(block, width)

    out = lax.dot_general(
        rows[...], w[...], (((1,), (1,)), ((), ())), preferred_element_type=F32
    )
    plus[...] = out[:block].astype(BF16)
    minus[...] = out[block : 2 * block].astype(BF16)
    across[...] = out[2 * block : 3 * block].astype(BF16)
    keep[...] = out[3 * block :]


def tokens_parts(where, own, other, w):
    n_y, per_row, width = own.shape
    block, depth = n_y * per_row // 2, w.shape[0]
    step = 256
    whole = pl.BlockSpec(own.shape, lambda n: (0, 0, 0))
    return pl.pallas_call(
        tokens_kernel,
        grid=(depth // step,),
        out_shape=[jax.ShapeDtypeStruct((block, depth), t) for t in (BF16, BF16, BF16, F32)],
        in_specs=[
            pl.BlockSpec(memory_space=pltpu.SMEM),
            whole,
            whole,
            pl.BlockSpec((step, width), lambda n: (n, 0)),
        ],
        out_specs=[pl.BlockSpec((block, step), lambda n: (0, n))] * 4,
        scratch_shapes=[pltpu.VMEM((4 * block, width), BF16)],
        compiler_params=pltpu.CompilerParams(vmem_limit_bytes=TOKENS_VMEM),
        cost_estimate=pl.CostEstimate(
            flops=8 * block * width * depth, bytes_accessed=6 * 1024 * 1024, transcendentals=0
        ),
        name="tokens_parts",
    )(where, own, other, w)


def weight_kernel(n, n_add, where, *refs):
    out, add, refs = refs[-1], refs[3 * n : -1], refs[: 3 * n]
    core = where[0]
    total = sum(r[...].astype(F32) for r in add) if n_add else None
    for i in range(n):
        t, mine, theirs = refs[3 * i : 3 * i + 3]
        depth = t.shape[-1]
        for half, g in ((core, mine), (1 - core, theirs)):
            part = lax.dot_general(
                t[:, half].reshape(g.shape[0], depth),
                g[...],
                (((0,), (0,)), ((), ())),
                preferred_element_type=F32,
            )
            total = part if total is None else total + part
    out[...] = total.astype(BF16)


def weight_part(where, terms, *adds):
    t, g = terms[0][0], terms[0][1]
    depth, width = t.shape[-1], g.shape[1]
    step = 512
    t_spec = pl.BlockSpec(t.shape, lambda n: (0, 0, 0, 0))
    g_spec = pl.BlockSpec((g.shape[0], step), lambda n: (0, n))
    out = pl.BlockSpec((depth, step), lambda n: (0, n))
    return pl.pallas_call(
        functools.partial(weight_kernel, len(terms), len(adds)),
        grid=(width // step,),
        out_shape=jax.ShapeDtypeStruct((depth, width), BF16),
        in_specs=[pl.BlockSpec(memory_space=pltpu.SMEM)]
        + [t_spec, g_spec, g_spec] * len(terms)
        + [out] * len(adds),
        out_specs=out,
        compiler_params=pltpu.CompilerParams(vmem_limit_bytes=VMEM_LIMIT),
        cost_estimate=pl.CostEstimate(
            flops=0,
            bytes_accessed=0,
            transcendentals=0,
        ),
        name="weight_part",
    )(where, *[a for term in terms for a in term], *adds)


def per_device(tokens, weight_up, d_hidden):
    n_dp, n_row, n_col = lax.axis_size("dp"), lax.axis_size("row"), lax.axis_size("col")
    n_y = n_row // 2
    depth, width = weight_up.shape
    core = lax.axis_index("row") % 2
    col = lax.axis_index("col")
    other_core = [(i, i ^ 1) for i in range(n_row)]
    y_groups = [[2 * y + c for y in range(n_y)] for c in range(2)]
    where = jnp.stack([core, col % 4, lax.axis_index("dp")]).astype(jnp.int32)

    panel = lax.all_gather(tokens, "col", axis=0, tiled=True)
    per_row = panel.shape[0] // n_row
    panel = panel.reshape(n_y, 2, per_row, depth)
    mine = lax.dynamic_index_in_dim(panel, core, 1, keepdims=False).reshape(-1, depth)
    theirs = lax.dynamic_index_in_dim(panel, 1 - core, 1, keepdims=False).reshape(-1, depth)

    got = lax.ppermute(
        jnp.dot(theirs, weight_up, preferred_element_type=F32).astype(BF16), "row", other_core
    )
    chip = jnp.dot(mine, weight_up, preferred_element_type=F32)
    chip = (chip + got.astype(F32)).astype(BF16)
    panel, chip = together((panel, chip))
    parts = lax.all_to_all(chip, "row", 0, 0, tiled=True, axis_index_groups=y_groups)

    t_up = lax.ppermute(panel, "dp", shift(n_dp, 1))
    t_down = lax.ppermute(panel, "dp", shift(n_dp, -1))

    pre = parts.reshape(n_y, per_row, width).astype(F32).sum(0)
    grad = gelu_back(pre, d_hidden)

    own = lax.all_gather(grad, "row", axis=0, tiled=True, axis_index_groups=y_groups)
    other = lax.ppermute(own, "row", other_core)
    up = lax.ppermute(own, "dp", shift(n_dp, 1))
    down = lax.ppermute(own, "dp", shift(n_dp, -1))

    other, t_up, t_down = together((other, t_up, t_down))

    plus, minus, across, keep = tokens_parts(
        where,
        own.reshape(n_y, per_row, width),
        other.reshape(n_y, per_row, width),
        weight_up,
    )
    plus = lax.ppermute(plus, "col", shift(n_col, 1))
    minus = lax.ppermute(minus, "col", shift(n_col, -1))
    across = lax.ppermute(across, "col", [(i, i ^ 2) for i in range(n_col)])

    up, down, plus, minus = together((up, down, plus, minus))
    far = lax.ppermute(down, "dp", shift(n_dp, -1))
    t_far = lax.ppermute(t_up, "dp", shift(n_dp, 1))
    up_other = lax.ppermute(up, "row", other_core)
    down_other = lax.ppermute(down, "row", other_core)

    quad = (keep + plus.astype(F32) + minus.astype(F32) + across.astype(F32)).astype(BF16)
    col_groups = [[c + 4 * q for q in range(n_col // 4)] for c in range(4)]
    parts = lax.all_to_all(quad, "col", 0, 0, tiled=True, axis_index_groups=col_groups)

    far_other = lax.ppermute(far, "row", other_core)
    d_weight = weight_part(
        where,
        [
            (panel, own, other),
            (t_up, up, up_other),
            (t_down, down, down_other),
            (t_far, far, far_other),
        ],
    )
    parts, d_weight = together((parts, d_weight))
    d_tokens = parts.reshape(n_col // 4, -1, depth).astype(F32).sum(0).astype(BF16)
    return d_tokens, d_weight


def solution(mesh):
    placed = (P(("dp", "col"), "row"), P("row", "col"), P(("dp", "row"), "col"))
    return jax.shard_map(
        per_device,
        mesh=mesh,
        in_specs=placed,
        out_specs=(P(("dp", "col"), "row"), P("row", "col")),
        check_vma=False,
    )
```

```python
import functools

import jax
import jax.numpy as jnp
from jax import lax
from jax.experimental import pallas as pl
from jax.experimental.pallas import tpu as pltpu
from jax.sharding import PartitionSpec as P

F32 = jnp.float32
BF16 = jnp.bfloat16
VMEM_LIMIT = 28 * 1024 * 1024
TOKENS_VMEM = 24 * 1024 * 1024


def gelu_back(pre, cot):
    value, pullback = jax.vjp(lambda v: jax.nn.gelu(v, approximate=True), pre)
    return pullback(cot.astype(F32))[0].astype(BF16)


def shift(n, step):
    return [(i, (i + step) % n) for i in range(n)]


together = lax.optimization_barrier


def tokens_kernel(where, own, other, w, plus, minus, across, keep, rows):
    core, k = where[0], where[1]
    n_y, per_row, width = own.shape
    half = per_row // 2
    block = n_y * half

    @pl.when(pl.program_id(0) == 0)
    def _():
        for i, step in enumerate((1, 3, 2, 0)):
            cls = lax.rem(k + step, 4)
            at = pl.ds(pl.multiple_of(lax.rem(cls, 2) * half, half), half)

            @pl.when(cls // 2 == core)
            def _():
                rows[pl.ds(i * block, block), :] = own[:, at, :].reshape(block, width)

            @pl.when(cls // 2 != core)
            def _():
                rows[pl.ds(i * block, block), :] = other[:, at, :].reshape(block, width)

    out = lax.dot_general(
        rows[...], w[...], (((1,), (1,)), ((), ())), preferred_element_type=F32
    )
    plus[...] = out[:block].astype(BF16)
    minus[...] = out[block : 2 * block].astype(BF16)
    across[...] = out[2 * block : 3 * block].astype(BF16)
    keep[...] = out[3 * block :]


def tokens_parts(where, own, other, w):
    n_y, per_row, width = own.shape
    block, depth = n_y * per_row // 2, w.shape[0]
    step = 256
    whole = pl.BlockSpec(own.shape, lambda n: (0, 0, 0))
    return pl.pallas_call(
        tokens_kernel,
        grid=(depth // step,),
        out_shape=[jax.ShapeDtypeStruct((block, depth), t) for t in (BF16, BF16, BF16, F32)],
        in_specs=[
            pl.BlockSpec(memory_space=pltpu.SMEM),
            whole,
            whole,
            pl.BlockSpec((step, width), lambda n: (n, 0)),
        ],
        out_specs=[pl.BlockSpec((block, step), lambda n: (0, n))] * 4,
        scratch_shapes=[pltpu.VMEM((4 * block, width), BF16)],
        compiler_params=pltpu.CompilerParams(vmem_limit_bytes=TOKENS_VMEM),
        cost_estimate=pl.CostEstimate(
            flops=8 * block * width * depth, bytes_accessed=6 * 1024 * 1024, transcendentals=0
        ),
        name="tokens_parts",
    )(where, own, other, w)


def weight_kernel(n, n_add, where, *refs):
    out, add, refs = refs[-1], refs[3 * n : -1], refs[: 3 * n]
    core = where[0]
    total = sum(r[...].astype(F32) for r in add) if n_add else None
    for i in range(n):
        t, mine, theirs = refs[3 * i : 3 * i + 3]
        depth = t.shape[-1]
        for half, g in ((core, mine), (1 - core, theirs)):
            part = lax.dot_general(
                t[:, half].reshape(g.shape[0], depth),
                g[...],
                (((0,), (0,)), ((), ())),
                preferred_element_type=F32,
            )
            total = part if total is None else total + part
    out[...] = total.astype(BF16)


def weight_part(where, terms, *adds):
    t, g = terms[0][0], terms[0][1]
    depth, width = t.shape[-1], g.shape[1]
    step = 512
    t_spec = pl.BlockSpec(t.shape, lambda n: (0, 0, 0, 0))
    g_spec = pl.BlockSpec((g.shape[0], step), lambda n: (0, n))
    out = pl.BlockSpec((depth, step), lambda n: (0, n))
    return pl.pallas_call(
        functools.partial(weight_kernel, len(terms), len(adds)),
        grid=(width // step,),
        out_shape=jax.ShapeDtypeStruct((depth, width), BF16),
        in_specs=[pl.BlockSpec(memory_space=pltpu.SMEM)]
        + [t_spec, g_spec, g_spec] * len(terms)
        + [out] * len(adds),
        out_specs=out,
        compiler_params=pltpu.CompilerParams(vmem_limit_bytes=VMEM_LIMIT),
        cost_estimate=pl.CostEstimate(
            flops=0,
            bytes_accessed=0,
            transcendentals=0,
        ),
        name="weight_part",
    )(where, *[a for term in terms for a in term], *adds)


def per_device(tokens, weight_up, d_hidden):
    n_dp, n_row, n_col = lax.axis_size("dp"), lax.axis_size("row"), lax.axis_size("col")
    n_y = n_row // 2
    depth, width = weight_up.shape
    core = lax.axis_index("row") % 2
    col = lax.axis_index("col")
    other_core = [(i, i ^ 1) for i in range(n_row)]
    y_groups = [[2 * y + c for y in range(n_y)] for c in range(2)]
    where = jnp.stack([core, col % 4, lax.axis_index("dp")]).astype(jnp.int32)

    panel = lax.all_gather(tokens, "col", axis=0, tiled=True)
    per_row = panel.shape[0] // n_row
    panel = panel.reshape(n_y, 2, per_row, depth)
    mine = lax.dynamic_index_in_dim(panel, core, 1, keepdims=False).reshape(-1, depth)
    theirs = lax.dynamic_index_in_dim(panel, 1 - core, 1, keepdims=False).reshape(-1, depth)

    got = lax.ppermute(
        jnp.dot(theirs, weight_up, preferred_element_type=F32).astype(BF16), "row", other_core
    )
    chip = jnp.dot(mine, weight_up, preferred_element_type=F32)
    chip = (chip + got.astype(F32)).astype(BF16)
    panel, chip = together((panel, chip))
    parts = lax.all_to_all(chip, "row", 0, 0, tiled=True, axis_index_groups=y_groups)

    t_up = lax.ppermute(panel, "dp", shift(n_dp, 1))
    t_down = lax.ppermute(panel, "dp", shift(n_dp, -1))

    pre = parts.reshape(n_y, per_row, width).astype(F32).sum(0)
    grad = gelu_back(pre, d_hidden)

    own = lax.all_gather(grad, "row", axis=0, tiled=True, axis_index_groups=y_groups)
    other = lax.ppermute(own, "row", other_core)
    up = lax.ppermute(own, "dp", shift(n_dp, 1))
    down = lax.ppermute(own, "dp", shift(n_dp, -1))

    other, t_up, t_down = together((other, t_up, t_down))

    plus, minus, across, keep = tokens_parts(
        where,
        own.reshape(n_y, per_row, width),
        other.reshape(n_y, per_row, width),
        weight_up,
    )
    plus = lax.ppermute(plus, "col", shift(n_col, 1))
    minus = lax.ppermute(minus, "col", shift(n_col, -1))
    across = lax.ppermute(across, "col", [(i, i ^ 2) for i in range(n_col)])

    up, down, plus, minus = together((up, down, plus, minus))
    far = lax.ppermute(down, "dp", shift(n_dp, -1))
    t_far = lax.ppermute(t_up, "dp", shift(n_dp, 1))
    up_other = lax.ppermute(up, "row", other_core)
    down_other = lax.ppermute(down, "row", other_core)

    quad = (keep + plus.astype(F32) + minus.astype(F32) + across.astype(F32)).astype(BF16)
    col_groups = [[c + 4 * q for q in range(n_col // 4)] for c in range(4)]
    parts = lax.all_to_all(quad, "col", 0, 0, tiled=True, axis_index_groups=col_groups)

    near = weight_part(
        where, [(panel, own, other), (t_up, up, up_other), (t_down, down, down_other)]
    )
    far, near, parts = together((far, near, parts))
    far_other = lax.ppermute(far, "row", other_core)
    d_weight = weight_part(where, [(t_far, far, far_other)], near)
    d_tokens = parts.reshape(n_col // 4, -1, depth).astype(F32).sum(0).astype(BF16)
    return d_tokens, d_weight


def solution(mesh):
    placed = (P(("dp", "col"), "row"), P("row", "col"), P(("dp", "row"), "col"))
    return jax.shard_map(
        per_device,
        mesh=mesh,
        in_specs=placed,
        out_specs=(P(("dp", "col"), "row"), P("row", "col")),
        check_vma=False,
    )
```

```python
import functools

import jax
import jax.numpy as jnp
from jax import lax
from jax.experimental import pallas as pl
from jax.experimental.pallas import tpu as pltpu
from jax.sharding import PartitionSpec as P

F32 = jnp.float32
BF16 = jnp.bfloat16
VMEM_LIMIT = 28 * 1024 * 1024
TOKENS_VMEM = 24 * 1024 * 1024


def gelu_back(pre, cot):
    value, pullback = jax.vjp(lambda v: jax.nn.gelu(v, approximate=True), pre)
    return pullback(cot.astype(F32))[0].astype(BF16)


def shift(n, step):
    return [(i, (i + step) % n) for i in range(n)]


together = lax.optimization_barrier


def tokens_kernel(where, own, other, w, plus, minus, across, keep, rows):
    core, k = where[0], where[1]
    n_y, per_row, width = own.shape
    half = per_row // 2
    block = n_y * half

    @pl.when(pl.program_id(0) == 0)
    def _():
        for i, step in enumerate((1, 3, 2, 0)):
            cls = lax.rem(k + step, 4)
            at = pl.ds(pl.multiple_of(lax.rem(cls, 2) * half, half), half)

            @pl.when(cls // 2 == core)
            def _():
                rows[pl.ds(i * block, block), :] = own[:, at, :].reshape(block, width)

            @pl.when(cls // 2 != core)
            def _():
                rows[pl.ds(i * block, block), :] = other[:, at, :].reshape(block, width)

    out = lax.dot_general(
        rows[...], w[...], (((1,), (1,)), ((), ())), preferred_element_type=F32
    )
    plus[...] = out[:block].astype(BF16)
    minus[...] = out[block : 2 * block].astype(BF16)
    across[...] = out[2 * block : 3 * block].astype(BF16)
    keep[...] = out[3 * block :]


def tokens_parts(where, own, other, w):
    n_y, per_row, width = own.shape
    block, depth = n_y * per_row // 2, w.shape[0]
    step = 256
    whole = pl.BlockSpec(own.shape, lambda n: (0, 0, 0))
    return pl.pallas_call(
        tokens_kernel,
        grid=(depth // step,),
        out_shape=[jax.ShapeDtypeStruct((block, depth), t) for t in (BF16, BF16, BF16, F32)],
        in_specs=[
            pl.BlockSpec(memory_space=pltpu.SMEM),
            whole,
            whole,
            pl.BlockSpec((step, width), lambda n: (n, 0)),
        ],
        out_specs=[pl.BlockSpec((block, step), lambda n: (0, n))] * 4,
        scratch_shapes=[pltpu.VMEM((4 * block, width), BF16)],
        compiler_params=pltpu.CompilerParams(vmem_limit_bytes=TOKENS_VMEM),
        cost_estimate=pl.CostEstimate(
            flops=8 * block * width * depth, bytes_accessed=6 * 1024 * 1024, transcendentals=0
        ),
        name="tokens_parts",
    )(where, own, other, w)


def weight_kernel(n, n_add, where, *refs):
    out, add, refs = refs[-1], refs[3 * n : -1], refs[: 3 * n]
    core = where[0]
    total = sum(r[...].astype(F32) for r in add) if n_add else None
    for i in range(n):
        t, mine, theirs = refs[3 * i : 3 * i + 3]
        depth = t.shape[-1]
        for half, g in ((core, mine), (1 - core, theirs)):
            part = lax.dot_general(
                t[:, half].reshape(g.shape[0], depth),
                g[...],
                (((0,), (0,)), ((), ())),
                preferred_element_type=F32,
            )
            total = part if total is None else total + part
    out[...] = total.astype(BF16)


def weight_part(where, terms, *adds):
    t, g = terms[0][0], terms[0][1]
    depth, width = t.shape[-1], g.shape[1]
    step = 512
    t_spec = pl.BlockSpec(t.shape, lambda n: (0, 0, 0, 0))
    g_spec = pl.BlockSpec((g.shape[0], step), lambda n: (0, n))
    out = pl.BlockSpec((depth, step), lambda n: (0, n))
    return pl.pallas_call(
        functools.partial(weight_kernel, len(terms), len(adds)),
        grid=(width // step,),
        out_shape=jax.ShapeDtypeStruct((depth, width), BF16),
        in_specs=[pl.BlockSpec(memory_space=pltpu.SMEM)]
        + [t_spec, g_spec, g_spec] * len(terms)
        + [out] * len(adds),
        out_specs=out,
        compiler_params=pltpu.CompilerParams(vmem_limit_bytes=VMEM_LIMIT),
        cost_estimate=pl.CostEstimate(
            flops=0,
            bytes_accessed=0,
            transcendentals=0,
        ),
        name="weight_part",
    )(where, *[a for term in terms for a in term], *adds)


def per_device(tokens, weight_up, d_hidden):
    n_dp, n_row, n_col = lax.axis_size("dp"), lax.axis_size("row"), lax.axis_size("col")
    n_y = n_row // 2
    depth, width = weight_up.shape
    core = lax.axis_index("row") % 2
    col = lax.axis_index("col")
    other_core = [(i, i ^ 1) for i in range(n_row)]
    y_groups = [[2 * y + c for y in range(n_y)] for c in range(2)]
    where = jnp.stack([core, col % 4, lax.axis_index("dp")]).astype(jnp.int32)

    panel = lax.all_gather(tokens, "col", axis=0, tiled=True)
    per_row = panel.shape[0] // n_row
    panel = panel.reshape(n_y, 2, per_row, depth)
    mine = lax.dynamic_index_in_dim(panel, core, 1, keepdims=False).reshape(-1, depth)
    theirs = lax.dynamic_index_in_dim(panel, 1 - core, 1, keepdims=False).reshape(-1, depth)

    got = lax.ppermute(
        jnp.dot(theirs, weight_up, preferred_element_type=F32).astype(BF16), "row", other_core
    )
    chip = jnp.dot(mine, weight_up, preferred_element_type=F32)
    chip = (chip + got.astype(F32)).astype(BF16)
    panel, chip = together((panel, chip))
    parts = lax.all_to_all(chip, "row", 0, 0, tiled=True, axis_index_groups=y_groups)

    t_up = lax.ppermute(panel, "dp", shift(n_dp, 1))
    t_down = lax.ppermute(panel, "dp", shift(n_dp, -1))

    pre = parts.reshape(n_y, per_row, width).astype(F32).sum(0)
    grad = gelu_back(pre, d_hidden)

    own = lax.all_gather(grad, "row", axis=0, tiled=True, axis_index_groups=y_groups)
    other = lax.ppermute(own, "row", other_core)
    up = lax.ppermute(own, "dp", shift(n_dp, 1))
    down = lax.ppermute(own, "dp", shift(n_dp, -1))

    other, t_up, t_down = together((other, t_up, t_down))

    plus, minus, across, keep = tokens_parts(
        where,
        own.reshape(n_y, per_row, width),
        other.reshape(n_y, per_row, width),
        weight_up,
    )
    plus = lax.ppermute(plus, "col", shift(n_col, 1))
    minus = lax.ppermute(minus, "col", shift(n_col, -1))
    across = lax.ppermute(across, "col", [(i, i ^ 2) for i in range(n_col)])

    up, down, plus, minus = together((up, down, plus, minus))
    far = lax.ppermute(down, "dp", shift(n_dp, -1))
    t_far = lax.ppermute(t_up, "dp", shift(n_dp, 1))
    up_other = lax.ppermute(up, "row", other_core)
    down_other = lax.ppermute(down, "row", other_core)

    quad = (keep + plus.astype(F32) + minus.astype(F32) + across.astype(F32)).astype(BF16)
    col_groups = [[c + 4 * q for q in range(n_col // 4)] for c in range(4)]
    parts = lax.all_to_all(quad, "col", 0, 0, tiled=True, axis_index_groups=col_groups)

    near = weight_part(
        where, [(panel, own, other), (t_up, up, up_other), (t_down, down, down_other)]
    )
    far, near, parts, t_far = together((far, near, parts, t_far))
    far_other = lax.ppermute(far, "row", other_core)
    d_weight = weight_part(where, [(t_far, far, far_other)], near)
    d_tokens = parts.reshape(n_col // 4, -1, depth).astype(F32).sum(0).astype(BF16)
    return d_tokens, d_weight


def solution(mesh):
    placed = (P(("dp", "col"), "row"), P("row", "col"), P(("dp", "row"), "col"))
    return jax.shard_map(
        per_device,
        mesh=mesh,
        in_specs=placed,
        out_specs=(P(("dp", "col"), "row"), P("row", "col")),
        check_vma=False,
    )
```
